32 devices in a mesh: adapter: 8 (over z, x), tensor: 4 (over y, core).
Axes of the slice: x: 2, y: 2, z: 4, core: 2. Of those that a mesh axis runs over, the one named last changes fastest.
Arguments:
- activations: bfloat16 [4096, 4096], P('adapter', 'tensor'), may hold values from -6 to 6
- output_gradient: bfloat16 [4096, 4096], P('adapter', 'tensor'), may hold values from -6 to 6
- frozen_weight: bfloat16 [4096, 4096], P(None, 'tensor'), may hold values from -0.09375 to 0.09375
- adapter_down_weight: bfloat16 [1024, 4096], P('adapter', 'tensor'), may hold values from -0.09375 to 0.09375
- adapter_up_weight: bfloat16 [1024, 4096], P('adapter', 'tensor'), may hold values from -0.09375 to 0.09375
- adapter_slot_table: int32 [64], replicated, may hold values from 0 to 63, as said below
- group_adapter_index: int32 [8, 6], P('adapter'), may hold values from 0 to 63, as said below
- group_token_length: int32 [8, 6], P('adapter'), may hold values from 1 to 128, as said below
Outputs:
- input_gradient: bfloat16 [4096, 4096], P('adapter', 'tensor')
- down_grad: float32 [1024, 4096], P('adapter', 'tensor')
- up_grad: float32 [1024, 4096], P('adapter', 'tensor')
The draws below stay inside these ranges and needn't reach their ends.
Inputs may be any that keep to these rules, and one draw needn't show every extreme that they name: `adapter_slot_table`: a permutation of the slots; slot k lies on adapter index k // 8. `group_adapter_index`: the adapters of one index's groups lie on distinct indices of the adapter axis; on every index one group of exactly 128 tokens uses an adapter stored on one index that is the same for all indices. `group_token_length`: each row sums to 512 and holds a group of exactly 128 tokens.
All inputs are finite; a program needn't handle non-finite values.
Results may differ from the reference program's by a relative error of at most 0.015.
Values may be sent and summed in bfloat16 or wider, within the bound.
No kernel may reach another device: no remote copies, remote signals or barrier semaphores. Data moves between devices by JAX's collectives and lax.ppermute only.
A program may use at most 128 MiB of HBM per device.

```python
import jax
import jax.numpy as jnp
from jax import lax

INPUT_FEATURES = 4096
OUTPUT_FEATURES = 4096
ADAPTER_RANK = 16
ADP_DEV = 8
TOK_DEV = 512
ADAPTER_TOTAL = 64
TOKENS = 4096
NGROUPS = 6
PEER_ROWS = 128
N_ADAPTER = 8
N_TENSOR = 4


def shared_layout(key):
    slot_perm = jax.random.permutation(jax.random.fold_in(key, 11), ADAPTER_TOTAL).astype(jnp.int32)
    hot_owner = jax.random.randint(jax.random.fold_in(key, 12), (), 0, N_ADAPTER).astype(jnp.int32)
    start_at = jax.random.randint(jax.random.fold_in(key, 13), (N_ADAPTER,), 0, NGROUPS).astype(jnp.int32)
    return (slot_perm, hot_owner, start_at)


def draw_adapter_slot_table(key, part):
    return shared_layout(key)[0]


def owner_row(row_key, hot_owner, start_at):
    others = jax.random.permutation(row_key, N_ADAPTER - 1).astype(jnp.int32)
    owners = jnp.concatenate([hot_owner[None], (hot_owner + 1 + others[:NGROUPS - 1]) % N_ADAPTER])
    return jnp.roll(owners, start_at)


def draw_group_adapter_index(key, part):
    slot_perm, hot_owner, start_at = shared_layout(key)
    inverse = jnp.argsort(slot_perm, stable=True).astype(jnp.int32)
    row_keys = jax.random.split(jax.random.fold_in(key, 14), N_ADAPTER)
    owners = jax.vmap(owner_row, in_axes=(0, None, 0))(row_keys, hot_owner, start_at)
    local_slot = jax.random.randint(jax.random.fold_in(key, 15), (N_ADAPTER, NGROUPS), 0, ADP_DEV).astype(jnp.int32)
    return inverse[owners * ADP_DEV + local_slot].astype(jnp.int32)


def draw_group_token_length(key, part):
    start_at = shared_layout(key)[2]
    remain = TOK_DEV - PEER_ROWS
    others = NGROUPS - 1
    common = remain // others
    spare = remain % others
    lowest = max(1 - common, common + 2 - PEER_ROWS)
    highest = min(common - 1, PEER_ROWS - common - 2)
    if lowest > 0 or highest < 0:
        lowest = 0
        highest = 0
    lengths = common + (jnp.arange(others) < spare).astype(jnp.int32)
    pairs = others // 2
    change = jax.random.randint(jax.random.fold_in(key, 16), (N_ADAPTER, pairs), lowest, highest + 1).astype(jnp.int32)
    signed = jnp.stack([change, -change], axis=2).reshape(N_ADAPTER, 2 * pairs)
    if others % 2 == 1:
        signed = jnp.concatenate([signed, jnp.zeros((N_ADAPTER, 1), jnp.int32)], axis=1)
    rest_rows = lengths[None, :] + signed
    full_rows = jnp.concatenate([jnp.full((N_ADAPTER, 1), PEER_ROWS, jnp.int32), rest_rows], axis=1)
    return jax.vmap(jnp.roll)(full_rows, start_at).astype(jnp.int32)


def block_levels(key, dims, cuts, low, top_value):
    gain, own = 1.0, jax.random.fold_in(key, 6)
    for axis_at, blocks in cuts:
        draws = jnp.exp(jax.random.uniform(jax.random.fold_in(own, axis_at), (blocks,), jnp.float32, low / len(cuts), top_value / len(cuts)))
        gain = gain * jnp.repeat(draws, dims[axis_at] // blocks).reshape([-1 if axis == axis_at else 1 for axis in range(len(dims))])
    return gain


def normal_values(own_key, shape, width, reach, shards=(), kind=jnp.bfloat16):
    gain = block_levels(own_key, shape, shards, -0.22, 0.18) if shards else 1.0
    drawn = jax.random.normal(own_key, shape, jnp.float32) * width * gain
    return jnp.minimum(jnp.maximum(drawn, -reach), reach).astype(kind)


def setup_inputs(seed: int = 0) -> dict:
    seeds = jax.random.split(jax.random.key(seed), 9)
    activations = normal_values(seeds[0], (TOKENS, INPUT_FEATURES), 1.0, 6.0, ((0, 8), (1, 4)))
    output_gradient = normal_values(seeds[1], (TOKENS, OUTPUT_FEATURES), 1.0, 6.0, ((0, 8), (1, 4)))
    frozen_weight = normal_values(seeds[2], (INPUT_FEATURES, OUTPUT_FEATURES), OUTPUT_FEATURES ** -0.5, 0.09375, ((1, 4),))
    adapter_down_weight = normal_values(seeds[3], (ADAPTER_TOTAL * ADAPTER_RANK, INPUT_FEATURES), INPUT_FEATURES ** -0.5, 0.09375, ((0, 8), (1, 4)))
    adapter_up_weight = normal_values(seeds[4], (ADAPTER_TOTAL * ADAPTER_RANK, OUTPUT_FEATURES), OUTPUT_FEATURES ** -0.5, 0.09375, ((0, 8), (1, 4)))
    adapter_slot_table = draw_adapter_slot_table(jax.random.fold_in(seeds[8], 71), 0)
    group_adapter_index = draw_group_adapter_index(jax.random.fold_in(seeds[8], 71), 0)
    group_token_length = draw_group_token_length(jax.random.fold_in(seeds[8], 71), 0)
    return dict(activations=activations, output_gradient=output_gradient, frozen_weight=frozen_weight, adapter_down_weight=adapter_down_weight, adapter_up_weight=adapter_up_weight, adapter_slot_table=adapter_slot_table, group_adapter_index=group_adapter_index, group_token_length=group_token_length)


adapter_scale = 2.0


def reference(activations, output_gradient, frozen_weight, adapter_down_weight, adapter_up_weight, adapter_slot_table, group_adapter_index, group_token_length):
    down_matrices = adapter_down_weight.reshape(ADAPTER_TOTAL, ADAPTER_RANK, INPUT_FEATURES)
    up_matrices = adapter_up_weight.reshape(ADAPTER_TOTAL, ADAPTER_RANK, OUTPUT_FEATURES)
    positions = jnp.arange(TOK_DEV, dtype=jnp.int32)
    block = OUTPUT_FEATURES // N_TENSOR

    def device_step(carry, device):
        grad_down, grad_up = carry
        input_rows_local = lax.dynamic_slice_in_dim(activations, device * TOK_DEV, TOK_DEV, 0)
        gradient_rows = lax.dynamic_slice_in_dim(output_gradient, device * TOK_DEV, TOK_DEV, 0)
        lengths = group_token_length[device]
        group_ends = jnp.cumsum(lengths).astype(jnp.int32)
        tok_group = jnp.sum((positions[:, None] >= group_ends[None, :]).astype(jnp.int32), axis=1)
        group_slots = adapter_slot_table[group_adapter_index[device]].astype(jnp.int32)
        tok_slot = group_slots[tok_group].astype(jnp.int32)
        down_block_rows = down_matrices[tok_slot].astype(jnp.float32)
        up_rows = up_matrices[tok_slot].astype(jnp.float32)
        down_proj = jnp.einsum("td,trd->tr", input_rows_local.astype(jnp.float32), down_block_rows)
        up_proj = jnp.einsum("td,trd->tr", gradient_rows.astype(jnp.float32), up_rows)
        down_reduced = down_proj.astype(jnp.bfloat16)
        up_reduced = up_proj.astype(jnp.bfloat16)
        adapter_input_grad = (adapter_scale * jnp.einsum("sp,spa->sa", up_reduced.astype(jnp.float32), down_block_rows)).astype(jnp.bfloat16)
        frozen_input_grad = jnp.zeros((TOK_DEV, INPUT_FEATURES), jnp.float32)
        for part in range(N_TENSOR):
            piece = jnp.dot(gradient_rows[:, part * block:(part + 1) * block], frozen_weight[:, part * block:(part + 1) * block].T, preferred_element_type=jnp.float32)
            frozen_input_grad = frozen_input_grad + piece.astype(jnp.bfloat16).astype(jnp.float32)
        input_token_rows = (frozen_input_grad + adapter_input_grad.astype(jnp.float32)).astype(jnp.bfloat16)
        down_outer_product = adapter_scale * up_reduced.astype(jnp.float32)[:, :, None] * input_rows_local.astype(jnp.float32)[:, None, :]
        up_outer_product = adapter_scale * down_reduced.astype(jnp.float32)[:, :, None] * gradient_rows.astype(jnp.float32)[:, None, :]
        grad_down = grad_down + jax.ops.segment_sum(down_outer_product, tok_slot, num_segments=ADAPTER_TOTAL)
        grad_up = grad_up + jax.ops.segment_sum(up_outer_product, tok_slot, num_segments=ADAPTER_TOTAL)
        return (grad_down, grad_up), input_token_rows

    start = (jnp.zeros((ADAPTER_TOTAL, ADAPTER_RANK, INPUT_FEATURES), jnp.float32), jnp.zeros((ADAPTER_TOTAL, ADAPTER_RANK, OUTPUT_FEATURES), jnp.float32))
    (grad_down, grad_up), rows = lax.scan(device_step, start, jnp.arange(N_ADAPTER, dtype=jnp.int32))
    return rows.reshape(TOKENS, INPUT_FEATURES), grad_down.reshape(ADAPTER_TOTAL * ADAPTER_RANK, INPUT_FEATURES), grad_up.reshape(ADAPTER_TOTAL * ADAPTER_RANK, OUTPUT_FEATURES)
```

```python
import functools

import jax
import jax.numpy as jnp
from jax import lax
from jax.experimental import pallas as pl
from jax.experimental.pallas import tpu as pltpu
from jax.sharding import PartitionSpec as P

RANK = 16
SLOTS = 8
SCALE = 2.0
LANES = 128
VMEM = pl.BlockSpec(memory_space=pltpu.VMEM)
SMEM = pl.BlockSpec(memory_space=pltpu.SMEM)
F32 = jnp.float32
BF16 = jnp.bfloat16
I32 = jnp.int32


def dot(a, b, ca, cb):
    return lax.dot_general(a, b, (((ca,), (cb,)), ((), ())), preferred_element_type=F32)


def exchange(x, axis, k):
    return lax.ppermute(x, axis, [(i, i ^ k) for i in range(lax.axis_size(axis))])


def sds(shape, dtype):
    return jax.ShapeDtypeStruct(shape, dtype)


def call(body, outs, n_vmem, n_smem=0, n_hbm=0, scratch=(), flops=0, moved=0, vmem=16):
    def run(*operands, after=()):
        tokens = len(after)
        at = n_smem + n_vmem + n_hbm

        def wrapped(*refs):
            body(*refs[:at], *refs[at + tokens :])

        return pl.pallas_call(
            wrapped,
            out_shape=outs,
            in_specs=[SMEM] * n_smem
            + [VMEM] * n_vmem
            + [pl.BlockSpec(memory_space=pltpu.HBM)] * n_hbm
            + [pl.BlockSpec(memory_space=pl.ANY)] * tokens,
            out_specs=jax.tree.map(lambda _: VMEM, outs),
            scratch_shapes=scratch,
            cost_estimate=pl.CostEstimate(flops=flops, bytes_accessed=moved, transcendentals=0),
            compiler_params=pltpu.CompilerParams(vmem_limit_bytes=vmem * 2**20),
        )(*operands, *after)

    return run


def request_body(n, groups, tokens, me_ref, slots_ref, index_ref, length_ref, asked_ref, offset_ref):
    me = me_ref[0]
    lane = lax.broadcasted_iota(I32, (n, LANES), 1)
    row = lax.broadcasted_iota(I32, (n, LANES), 0)
    token = lax.broadcasted_iota(I32, (SLOTS, tokens), 1)
    asked = jnp.zeros((n, LANES), I32)
    offset = jnp.zeros((SLOTS, tokens), I32)
    end = jnp.int32(0)
    for g in range(groups):
        slot = slots_ref[index_ref[0, g]]
        owner = lax.shift_right_logical(slot, 3)
        local = jnp.bitwise_and(slot, SLOTS - 1)
        asked = jnp.where((lane == owner) & (row == me), local + 1, asked)
        offset = jnp.where(token >= end, jnp.bitwise_xor(owner, me), offset)
        end = end + length_ref[0, g]
    asked_ref[...] = asked
    offset_ref[...] = offset


def wanted(me, k, table):
    lane = lax.broadcasted_iota(I32, table.shape, 1)
    row = lax.broadcasted_iota(I32, table.shape, 0)
    mine = jnp.where((lane == me) & (row == jnp.bitwise_xor(me, k)), table, 0)
    return jnp.sum(jnp.sum(mine, axis=1, keepdims=True), axis=0, keepdims=True)


def select_body(ks, me_ref, table_ref, down_ref, up_ref, *out_refs):
    me = me_ref[0]
    table = table_ref[...]
    rows = SLOTS * RANK
    col = lax.broadcasted_iota(I32, (RANK, rows), 1)
    row = lax.broadcasted_iota(I32, (RANK, rows), 0)
    picks = [
        (col == (wanted(me, k, table) - 1) * RANK + row).astype(F32).astype(BF16) for k in ks
    ]
    pick = jnp.concatenate(picks, axis=0)
    up = dot(pick, up_ref[...], 1, 0).astype(BF16)
    down = dot(pick, down_ref[...], 1, 0).astype(BF16)
    for i in range(len(ks)):
        out_refs[i][pl.ds(0, RANK), :] = up[i * RANK : (i + 1) * RANK]
        out_refs[i][pl.ds(RANK, RANK), :] = down[i * RANK : (i + 1) * RANK]


def project_body(ks, offset_ref, x_ref, g_ref, *refs):
    map_refs, out_ref = refs[: len(ks)], refs[len(ks)]
    offset = offset_ref[0:1, :]
    up_maps = jnp.concatenate([m[pl.ds(0, RANK), :] for m in map_refs], axis=0)
    down_maps = jnp.concatenate([m[pl.ds(RANK, RANK), :] for m in map_refs], axis=0)
    up_wide = dot(up_maps, g_ref[...], 1, 1)
    down_wide = dot(down_maps, x_ref[...], 1, 1)
    up = jnp.zeros((RANK, up_wide.shape[1]), F32)
    down = up
    for i, k in enumerate(ks):
        mask = offset == k
        up = up + jnp.where(mask, up_wide[i * RANK : (i + 1) * RANK], 0.0)
        down = down + jnp.where(mask, down_wide[i * RANK : (i + 1) * RANK], 0.0)
    out_ref[pl.ds(0, RANK), :] = up.astype(BF16)
    out_ref[pl.ds(RANK, RANK), :] = down.astype(BF16)


def spread(ks, offset, low):
    zero = jnp.zeros_like(low)
    return jnp.concatenate([jnp.where(offset == k, low, zero) for k in ks], axis=0).astype(BF16)


def gradient_body(ks, parts, offset_ref, x_ref, g_ref, *refs):
    part_refs, out_refs, low_ref = refs[:parts], refs[parts : parts + len(ks)], refs[-1]
    offset = offset_ref[0:1, :]
    total = part_refs[0][...].astype(F32)
    for p in part_refs[1:]:
        total = total + p[...].astype(F32)
    total = total.astype(BF16)
    low_ref[...] = total
    total = total.astype(F32)
    up_wide = spread(ks, offset, total[:RANK])
    down_wide = spread(ks, offset, total[RANK:])
    down_grad = (SCALE * dot(up_wide, x_ref[...], 1, 0)).astype(BF16)
    up_grad = (SCALE * dot(down_wide, g_ref[...], 1, 0)).astype(BF16)
    for i in range(len(ks)):
        out_refs[i][pl.ds(0, RANK), :] = down_grad[i * RANK : (i + 1) * RANK]
        out_refs[i][pl.ds(RANK, RANK), :] = up_grad[i * RANK : (i + 1) * RANK]


def collect_body(ks, me_ref, table_ref, *refs):
    in_refs, down_ref, up_ref = refs[: len(ks)], refs[-2], refs[-1]
    me = me_ref[0]
    table = table_ref[...]
    rows = SLOTS * RANK
    row = lax.broadcasted_iota(I32, (rows, RANK), 0)
    col = lax.broadcasted_iota(I32, (rows, RANK), 1)
    place = jnp.concatenate(
        [(row == (wanted(me, k, table) - 1) * RANK + col).astype(F32).astype(BF16) for k in ks], axis=1
    )
    down = jnp.concatenate([r[pl.ds(0, RANK), :] for r in in_refs], axis=0)
    up = jnp.concatenate([r[pl.ds(RANK, RANK), :] for r in in_refs], axis=0)
    down_ref[...] = dot(place, down, 1, 0)
    up_ref[...] = dot(place, up, 1, 0)


def base_body(tile, at_ref, g_ref, w_ref, out_ref, held, sems):
    width = out_ref.shape[1]
    first = at_ref[0] * width
    copies = [
        pltpu.make_async_copy(
            w_ref.at[pl.ds(pl.multiple_of(first + i * tile, tile), tile), :], held.at[i], sems.at[i]
        )
        for i in range(width // tile)
    ]
    for c in copies:
        c.start()
    for i, c in enumerate(copies):
        c.wait()
        out_ref[:, pl.ds(i * tile, tile)] = dot(g_ref[...], held[i], 1, 1).astype(BF16)


def base_product(gradient, weight, at, width, after=(), tile=512):
    tokens, depth = gradient.shape
    tiles = width // tile
    return call(
        functools.partial(base_body, tile),
        sds((tokens, width), BF16),
        1,
        1,
        1,
        scratch=[pltpu.VMEM((tiles, tile, depth), BF16), pltpu.SemaphoreType.DMA((tiles,))],
        flops=2 * tokens * depth * width,
        moved=2 * depth * width,
    )(at, gradient, weight, after=after)


def add_body(a_ref, b_ref, out_ref):
    out_ref[...] = (a_ref[...].astype(F32) + b_ref[...].astype(F32)).astype(BF16)


def lora_body(ks, offset_ref, low_ref, *refs):
    map_refs, term_refs, out_ref = refs[: len(ks)], refs[len(ks) : -1], refs[-1]
    down_maps = jnp.concatenate([m[pl.ds(RANK, RANK), :] for m in map_refs], axis=0)
    up_wide = spread(ks, offset_ref[0:1, :], low_ref[pl.ds(0, RANK), :].astype(F32))
    total = (SCALE * dot(up_wide, down_maps, 0, 0)).astype(BF16).astype(F32)
    for t in term_refs:
        total = total + t[...].astype(F32)
    out_ref[...] = total


def finish_body(a_ref, b_ref, out_ref, token_ref):
    out_ref[...] = (a_ref[...] + b_ref[...].astype(F32)).astype(BF16)
    token_ref[...] = jnp.zeros_like(token_ref)


def on_device(x, g, weight, down_maps, up_maps, slot_table, group_index, group_length):
    tokens, width = x.shape
    n = lax.axis_size("adapter")
    tensor = lax.axis_size("tensor")
    groups = group_index.shape[1]
    ks = tuple(range(n))
    weight, slot_table, group_index, group_length = (
        pltpu.with_memory_space_constraint(a, pltpu.HBM)
        for a in (weight, slot_table, group_index, group_length)
    )
    me = lax.axis_index("adapter").astype(I32).reshape(1)
    part = lax.axis_index("tensor").astype(I32)

    asked, offset = call(
        functools.partial(request_body, n, groups, tokens),
        (sds((n, LANES), I32), sds((SLOTS, tokens), I32)),
        0,
        4,
    )(me, slot_table, group_index, group_length)

    def product(k, *after):
        return base_product(g, weight, jnp.bitwise_xor(part, k).reshape(1), width, after)

    table = asked
    far_other = product(3, asked)
    far_got = exchange(far_other, "tensor", 1)
    table = table + exchange(table, "adapter", n // 2)
    far_own = product(2, far_other, table)
    k = n // 4
    while k:
        table = table + exchange(table, "adapter", k)
        k //= 2
    wide = sds((tokens, width), BF16)
    far_sum = call(add_body, wide, 2)(far_own, far_got)
    across = exchange(far_sum, "tensor", 2)
    sent = call(
        functools.partial(select_body, ks),
        tuple(sds((2 * RANK, width), BF16) for _ in ks),
        3,
        1,
    )(me, table, down_maps, up_maps, after=(far_sum,))
    order = sorted(ks[1:], key=lambda k: (k < n // 2, k))
    got = {k: exchange(sent[k], "adapter", k) for k in order}
    near_other = product(1, sent[0])
    near_got = exchange(near_other, "tensor", 1)
    near_own = product(0, near_other)
    maps = [sent[0]] + [got[k] for k in ks[1:]]
    own_part = call(
        functools.partial(project_body, ks), sds((2 * RANK, tokens), BF16), 3 + n
    )(offset, x, g, *maps, after=(near_own,))
    parts = [own_part] + [exchange(own_part, "tensor", k) for k in range(1, tensor)]
    out = call(
        functools.partial(gradient_body, ks, tensor),
        tuple(sds((2 * RANK, width), BF16) for _ in ks) + (sds((2 * RANK, tokens), BF16),),
        3 + tensor,
    )(offset, x, g, *parts)
    low = out[-1]
    got = {k: exchange(out[k], "adapter", k) for k in order}
    back = [out[0]] + [got[k] for k in ks[1:]]
    near = call(functools.partial(lora_body, ks), sds((tokens, width), F32), 2 + n + 2)(
        offset, low, *maps, near_own, near_got
    )
    input_gradient, finished = call(finish_body, (wide, sds((8, LANES), F32)), 2)(near, across)
    down_grad, up_grad = call(
        functools.partial(collect_body, ks),
        (sds((SLOTS * RANK, width), F32), sds((SLOTS * RANK, width), F32)),
        1 + n,
        1,
    )(me, table, *back, after=(finished,))
    return input_gradient, down_grad, up_grad


def solution(mesh):
    in_specs = (
        P("adapter", "tensor"),
        P("adapter", "tensor"),
        P(None, "tensor"),
        P("adapter", "tensor"),
        P("adapter", "tensor"),
        P(),
        P("adapter", None),
        P("adapter", None),
    )
    out_specs = (P("adapter", "tensor"), P("adapter", "tensor"), P("adapter", "tensor"))
    return jax.shard_map(
        on_device, mesh=mesh, in_specs=in_specs, out_specs=out_specs, check_vma=False
    )
```

```python
import functools

import jax
import jax.numpy as jnp
from jax import lax
from jax.experimental import pallas as pl
from jax.experimental.pallas import tpu as pltpu
from jax.sharding import PartitionSpec as P

RANK = 16
SLOTS = 8
SCALE = 2.0
LANES = 128
VMEM = pl.BlockSpec(memory_space=pltpu.VMEM)
SMEM = pl.BlockSpec(memory_space=pltpu.SMEM)
F32 = jnp.float32
BF16 = jnp.bfloat16
I32 = jnp.int32


def dot(a, b, ca, cb):
    return lax.dot_general(a, b, (((ca,), (cb,)), ((), ())), preferred_element_type=F32)


def exchange(x, axis, k):
    return lax.ppermute(x, axis, [(i, i ^ k) for i in range(lax.axis_size(axis))])


def sds(shape, dtype):
    return jax.ShapeDtypeStruct(shape, dtype)


def call(body, outs, n_vmem, n_smem=0, n_hbm=0, scratch=(), flops=0, moved=0, vmem=16):
    def run(*operands, after=()):
        tokens = len(after)
        at = n_smem + n_vmem + n_hbm

        def wrapped(*refs):
            body(*refs[:at], *refs[at + tokens :])

        return pl.pallas_call(
            wrapped,
            name=getattr(body, "func", body).__name__,
            out_shape=outs,
            in_specs=[SMEM] * n_smem
            + [VMEM] * n_vmem
            + [pl.BlockSpec(memory_space=pltpu.HBM)] * n_hbm
            + [pl.BlockSpec(memory_space=pl.ANY)] * tokens,
            out_specs=jax.tree.map(lambda _: VMEM, outs),
            scratch_shapes=scratch,
            cost_estimate=pl.CostEstimate(flops=flops, bytes_accessed=moved, transcendentals=0),
            compiler_params=pltpu.CompilerParams(vmem_limit_bytes=vmem * 2**20),
        )(*operands, *after)

    return run


def request_body(n, groups, tokens, me_ref, slots_ref, index_ref, length_ref, asked_ref, offset_ref):
    me = me_ref[0]
    lane = lax.broadcasted_iota(I32, (n, LANES), 1)
    row = lax.broadcasted_iota(I32, (n, LANES), 0)
    token = lax.broadcasted_iota(I32, (SLOTS, tokens), 1)
    asked = jnp.zeros((n, LANES), I32)
    offset = jnp.zeros((SLOTS, tokens), I32)
    end = jnp.int32(0)
    for g in range(groups):
        slot = slots_ref[index_ref[0, g]]
        owner = lax.shift_right_logical(slot, 3)
        local = jnp.bitwise_and(slot, SLOTS - 1)
        asked = jnp.where((lane == owner) & (row == me), local + 1, asked)
        offset = jnp.where(token >= end, jnp.bitwise_xor(owner, me), offset)
        end = end + length_ref[0, g]
    asked_ref[...] = asked
    offset_ref[...] = offset


def wanted(me, k, table):
    lane = lax.broadcasted_iota(I32, table.shape, 1)
    row = lax.broadcasted_iota(I32, table.shape, 0)
    mine = jnp.where((lane == me) & (row == jnp.bitwise_xor(me, k)), table, 0)
    return jnp.sum(jnp.sum(mine, axis=1, keepdims=True), axis=0, keepdims=True)


def select_body(ks, me_ref, table_ref, down_ref, up_ref, *out_refs):
    me = me_ref[0]
    table = table_ref[...]
    rows = SLOTS * RANK
    col = lax.broadcasted_iota(I32, (RANK, rows), 1)
    row = lax.broadcasted_iota(I32, (RANK, rows), 0)
    picks = [
        (col == (wanted(me, k, table) - 1) * RANK + row).astype(F32).astype(BF16) for k in ks
    ]
    pick = jnp.concatenate(picks, axis=0)
    up = dot(pick, up_ref[...], 1, 0).astype(BF16)
    down = dot(pick, down_ref[...], 1, 0).astype(BF16)
    for i in range(len(ks)):
        out_refs[i][pl.ds(0, RANK), :] = up[i * RANK : (i + 1) * RANK]
        out_refs[i][pl.ds(RANK, RANK), :] = down[i * RANK : (i + 1) * RANK]


def project_body(ks, offset_ref, x_ref, g_ref, *refs):
    map_refs, out_ref = refs[: len(ks)], refs[len(ks)]
    offset = offset_ref[0:1, :]
    up_maps = jnp.concatenate([m[pl.ds(0, RANK), :] for m in map_refs], axis=0)
    down_maps = jnp.concatenate([m[pl.ds(RANK, RANK), :] for m in map_refs], axis=0)
    up_wide = dot(up_maps, g_ref[...], 1, 1)
    down_wide = dot(down_maps, x_ref[...], 1, 1)
    up = jnp.zeros((RANK, up_wide.shape[1]), F32)
    down = up
    for i, k in enumerate(ks):
        mask = offset == k
        up = up + jnp.where(mask, up_wide[i * RANK : (i + 1) * RANK], 0.0)
        down = down + jnp.where(mask, down_wide[i * RANK : (i + 1) * RANK], 0.0)
    out_ref[pl.ds(0, RANK), :] = up.astype(BF16)
    out_ref[pl.ds(RANK, RANK), :] = down.astype(BF16)


def spread(ks, offset, low):
    zero = jnp.zeros_like(low)
    return jnp.concatenate([jnp.where(offset == k, low, zero) for k in ks], axis=0).astype(BF16)


def gradient_body(ks, parts, offset_ref, x_ref, g_ref, *refs):
    part_refs, out_refs, low_ref = refs[:parts], refs[parts : parts + len(ks)], refs[-1]
    offset = offset_ref[0:1, :]
    total = part_refs[0][...].astype(F32)
    for p in part_refs[1:]:
        total = total + p[...].astype(F32)
    total = total.astype(BF16)
    low_ref[...] = total
    total = total.astype(F32)
    up_wide = spread(ks, offset, total[:RANK])
    down_wide = spread(ks, offset, total[RANK:])
    down_grad = (SCALE * dot(up_wide, x_ref[...], 1, 0)).astype(BF16)
    up_grad = (SCALE * dot(down_wide, g_ref[...], 1, 0)).astype(BF16)
    for i in range(len(ks)):
        out_refs[i][pl.ds(0, RANK), :] = down_grad[i * RANK : (i + 1) * RANK]
        out_refs[i][pl.ds(RANK, RANK), :] = up_grad[i * RANK : (i + 1) * RANK]


def collect_body(ks, me_ref, table_ref, *refs):
    in_refs, down_ref, up_ref = refs[: len(ks)], refs[-2], refs[-1]
    me = me_ref[0]
    table = table_ref[...]
    rows = SLOTS * RANK
    row = lax.broadcasted_iota(I32, (rows, RANK), 0)
    col = lax.broadcasted_iota(I32, (rows, RANK), 1)
    place = jnp.concatenate(
        [(row == (wanted(me, k, table) - 1) * RANK + col).astype(F32).astype(BF16) for k in ks], axis=1
    )
    down = jnp.concatenate([r[pl.ds(0, RANK), :] for r in in_refs], axis=0)
    up = jnp.concatenate([r[pl.ds(RANK, RANK), :] for r in in_refs], axis=0)
    down_ref[...] = dot(place, down, 1, 0)
    up_ref[...] = dot(place, up, 1, 0)


def base_body(tile, loads, adds, at_ref, *refs):
    refs = list(refs)
    if not loads:
        g = refs.pop(0)
    w_ref = refs.pop(0)
    late = refs[: loads + adds]
    out_ref, *inner, held, sems = refs[loads + adds :]
    width = out_ref.shape[1]
    first = at_ref[0] * width
    copies = [
        pltpu.make_async_copy(
            w_ref.at[pl.ds(pl.multiple_of(first + i * tile, tile), tile), :], held.at[i], sems.at[i]
        )
        for i in range(width // tile)
    ]
    others = [
        pltpu.make_async_copy(a, inner[i], sems.at[len(copies) + i]) for i, a in enumerate(late)
    ]
    if loads:
        others[0].start()
        g = inner[0]
    for c in copies:
        c.start()
    for c in others[loads:]:
        c.start()
    if loads:
        others[0].wait()
    for i, c in enumerate(copies):
        c.wait()
        columns = pl.ds(i * tile, tile)
        total = dot(g[...], held[i], 1, 1).astype(BF16)
        if i == 0:
            for o in others[loads:]:
                o.wait()
        for t in inner[loads:]:
            total = (total.astype(F32) + t[:, columns].astype(F32)).astype(BF16)
        out_ref[:, columns] = total


def base_product(gradient, weight, at, width, terms=(), loads=False, after=(), tile=512):
    tokens, depth = gradient.shape
    tiles = width // tile
    late = (gradient,) * loads + terms
    return call(
        functools.partial(base_body, tile, int(loads), len(terms)),
        sds((tokens, width), BF16),
        int(not loads),
        1,
        1 + len(late),
        scratch=[pltpu.VMEM((tokens, depth), BF16)] * len(late)
        + [pltpu.VMEM((tiles, tile, depth), BF16), pltpu.SemaphoreType.DMA((tiles + len(late),))],
        flops=2 * tokens * depth * width,
        moved=2 * depth * width,
        vmem=8,
    )(at, *((gradient,) * (not loads)), weight, *late, after=after)


def finish_body(ks, rows, offset_ref, low_ref, *refs):
    map_refs, term_refs, (out_ref, token_ref) = refs[: len(ks)], refs[len(ks) : -2], refs[-2:]
    down_maps = jnp.concatenate([m[pl.ds(RANK, RANK), :] for m in map_refs], axis=0)
    for first in range(0, out_ref.shape[0], rows):
        at = pl.ds(first, rows)
        up_wide = spread(ks, offset_ref[0:1, at], low_ref[pl.ds(0, RANK), at].astype(F32))
        lora = (SCALE * dot(up_wide, down_maps, 0, 0)).astype(BF16).astype(F32)
        total = term_refs[0][at, :].astype(F32)
        for t in term_refs[1:]:
            total = total + t[at, :].astype(F32)
        out_ref[at, :] = (total + lora).astype(BF16)
    token_ref[...] = jnp.zeros_like(token_ref)


def on_device(x, g, weight, down_maps, up_maps, slot_table, group_index, group_length):
    tokens, width = x.shape
    n = lax.axis_size("adapter")
    tensor = lax.axis_size("tensor")
    groups = group_index.shape[1]
    ks = tuple(range(n - 1, n // 2 - 1, -1)) + (0,) + tuple(range(n // 2 - 1, 0, -1))
    weight, slot_table, group_index, group_length, g_hbm = (
        pltpu.with_memory_space_constraint(a, pltpu.HBM)
        for a in (weight, slot_table, group_index, group_length, g)
    )
    me = lax.axis_index("adapter").astype(I32).reshape(1)
    part = lax.axis_index("tensor").astype(I32)

    asked, offset = call(
        functools.partial(request_body, n, groups, tokens),
        (sds((n, LANES), I32), sds((SLOTS, tokens), I32)),
        0,
        4,
    )(me, slot_table, group_index, group_length)

    def product(k, *after, terms=(), loads=False):
        at = jnp.bitwise_xor(part, k).reshape(1)
        terms = tuple(pltpu.with_memory_space_constraint(t, pltpu.HBM) for t in terms)
        return base_product(g_hbm if loads else g, weight, at, width, terms, loads, after)

    wide = sds((tokens, width), BF16)
    table, tables, hop = asked, [], n // 2
    while hop:
        table = table + exchange(table, "adapter", hop)
        tables.append(table)
        hop //= 2
    far_other = product(3, asked, loads=True)
    far_got = exchange(far_other, "tensor", 1)
    near_other = product(1, far_other, loads=False)
    near_got = exchange(near_other, "tensor", 1)
    far_sum = product(2, tables[0], terms=(far_got,), loads=True)
    across = exchange(far_sum, "tensor", 2)
    sent = call(
        functools.partial(select_body, ks),
        tuple(sds((2 * RANK, width), BF16) for _ in ks),
        3,
        1,
    )(me, table, down_maps, up_maps, after=(far_sum,))
    order = [k for k in ks if k]
    sent = dict(zip(ks, sent))
    got = {k: exchange(sent[k], "adapter", k) for k in order}
    got[0] = sent[0]
    maps = [got[k] for k in ks]
    own_part = call(
        functools.partial(project_body, ks), sds((2 * RANK, tokens), BF16), 3 + n, flops=5000000000
    )(offset, x, g, *maps, after=())
    parts = [own_part] + [exchange(own_part, "tensor", k) for k in range(1, tensor)]
    out = call(
        functools.partial(gradient_body, ks, tensor),
        tuple(sds((2 * RANK, width), BF16) for _ in ks) + (sds((2 * RANK, tokens), BF16),),
        3 + tensor,
        flops=5000000000,
    )(offset, x, g, *parts, after=(across,))
    low = out[-1]
    sums = dict(zip(ks, out))
    got = {k: exchange(sums[k], "adapter", k) for k in order}
    got[0] = sums[0]
    back = [got[k] for k in ks]
    near_sum = product(0, out[-1], terms=(near_got,), loads=False)
    input_gradient, finished = call(
        functools.partial(finish_body, ks, 256), (wide, sds((8, LANES), F32)), 2 + n + 2
    )(offset, low, *maps, near_sum, across)
    down_grad, up_grad = call(
        functools.partial(collect_body, ks),
        (sds((SLOTS * RANK, width), F32), sds((SLOTS * RANK, width), F32)),
        1 + n,
        1,
    )(me, table, *back, after=(finished,))
    return input_gradient, down_grad, up_grad


def solution(mesh):
    in_specs = (
        P("adapter", "tensor"),
        P("adapter", "tensor"),
        P(None, "tensor"),
        P("adapter", "tensor"),
        P("adapter", "tensor"),
        P(),
        P("adapter", None),
        P("adapter", None),
    )
    out_specs = (P("adapter", "tensor"), P("adapter", "tensor"), P("adapter", "tensor"))
    return jax.shard_map(
        on_device, mesh=mesh, in_specs=in_specs, out_specs=out_specs, check_vma=False
    )
```

```python
import functools

import jax
import jax.numpy as jnp
from jax import lax
from jax.experimental import pallas as pl
from jax.experimental.pallas import tpu as pltpu
from jax.sharding import PartitionSpec as P

RANK = 16
SLOTS = 8
SCALE = 2.0
LANES = 128
VMEM = pl.BlockSpec(memory_space=pltpu.VMEM)
SMEM = pl.BlockSpec(memory_space=pltpu.SMEM)
F32 = jnp.float32
BF16 = jnp.bfloat16
I32 = jnp.int32


def dot(a, b, ca, cb):
    return lax.dot_general(a, b, (((ca,), (cb,)), ((), ())), preferred_element_type=F32)


def exchange(x, axis, k):
    return lax.ppermute(x, axis, [(i, i ^ k) for i in range(lax.axis_size(axis))])


def sds(shape, dtype):
    return jax.ShapeDtypeStruct(shape, dtype)


def call(body, outs, n_vmem, n_smem=0, n_hbm=0, scratch=(), flops=0, moved=0, vmem=16):
    def run(*operands, after=()):
        tokens = len(after)
        at = n_smem + n_vmem + n_hbm

        def wrapped(*refs):
            body(*refs[:at], *refs[at + tokens :])

        return pl.pallas_call(
            wrapped,
            name=getattr(body, "func", body).__name__,
            out_shape=outs,
            in_specs=[SMEM] * n_smem
            + [VMEM] * n_vmem
            + [pl.BlockSpec(memory_space=pltpu.HBM)] * n_hbm
            + [pl.BlockSpec(memory_space=pl.ANY)] * tokens,
            out_specs=jax.tree.map(lambda _: VMEM, outs),
            scratch_shapes=scratch,
            cost_estimate=pl.CostEstimate(flops=flops, bytes_accessed=moved, transcendentals=0),
            compiler_params=pltpu.CompilerParams(vmem_limit_bytes=vmem * 2**20),
        )(*operands, *after)

    return run


def request_body(n, groups, tokens, me_ref, slots_ref, index_ref, length_ref, asked_ref, offset_ref):
    me = me_ref[0]
    lane = lax.broadcasted_iota(I32, (n, LANES), 1)
    row = lax.broadcasted_iota(I32, (n, LANES), 0)
    token = lax.broadcasted_iota(I32, (SLOTS, tokens), 1)
    asked = jnp.zeros((n, LANES), I32)
    offset = jnp.zeros((SLOTS, tokens), I32)
    end = jnp.int32(0)
    for g in range(groups):
        slot = slots_ref[index_ref[0, g]]
        owner = lax.shift_right_logical(slot, 3)
        local = jnp.bitwise_and(slot, SLOTS - 1)
        asked = jnp.where((lane == owner) & (row == me), local + 1, asked)
        offset = jnp.where(token >= end, jnp.bitwise_xor(owner, me), offset)
        end = end + length_ref[0, g]
    asked_ref[...] = asked
    offset_ref[...] = offset


def wanted(me, k, table):
    lane = lax.broadcasted_iota(I32, table.shape, 1)
    row = lax.broadcasted_iota(I32, table.shape, 0)
    mine = jnp.where((lane == me) & (row == jnp.bitwise_xor(me, k)), table, 0)
    return jnp.sum(jnp.sum(mine, axis=1, keepdims=True), axis=0, keepdims=True)


def select_body(ks, me_ref, table_ref, down_ref, up_ref, *out_refs):
    me = me_ref[0]
    table = table_ref[...]
    rows = SLOTS * RANK
    col = lax.broadcasted_iota(I32, (RANK, rows), 1)
    row = lax.broadcasted_iota(I32, (RANK, rows), 0)
    picks = [
        (col == (wanted(me, k, table) - 1) * RANK + row).astype(F32).astype(BF16) for k in ks
    ]
    pick = jnp.concatenate(picks, axis=0)
    up = dot(pick, up_ref[...], 1, 0).astype(BF16)
    down = dot(pick, down_ref[...], 1, 0).astype(BF16)
    for i in range(len(ks)):
        out_refs[i][pl.ds(0, RANK), :] = up[i * RANK : (i + 1) * RANK]
        out_refs[i][pl.ds(RANK, RANK), :] = down[i * RANK : (i + 1) * RANK]


def project_body(ks, offset_ref, x_ref, g_ref, *refs):
    map_refs, out_ref = refs[: len(ks)], refs[len(ks)]
    offset = offset_ref[0:1, :]
    up_maps = jnp.concatenate([m[pl.ds(0, RANK), :] for m in map_refs], axis=0)
    down_maps = jnp.concatenate([m[pl.ds(RANK, RANK), :] for m in map_refs], axis=0)
    up_wide = dot(up_maps, g_ref[...], 1, 1)
    down_wide = dot(down_maps, x_ref[...], 1, 1)
    up = jnp.zeros((RANK, up_wide.shape[1]), F32)
    down = up
    for i, k in enumerate(ks):
        mask = offset == k
        up = up + jnp.where(mask, up_wide[i * RANK : (i + 1) * RANK], 0.0)
        down = down + jnp.where(mask, down_wide[i * RANK : (i + 1) * RANK], 0.0)
    out_ref[pl.ds(0, RANK), :] = up.astype(BF16)
    out_ref[pl.ds(RANK, RANK), :] = down.astype(BF16)


def spread(ks, offset, low):
    zero = jnp.zeros_like(low)
    return jnp.concatenate([jnp.where(offset == k, low, zero) for k in ks], axis=0).astype(BF16)


def gradient_body(ks, parts, offset_ref, x_ref, g_ref, *refs):
    part_refs, out_refs, low_ref = refs[:parts], refs[parts : parts + len(ks)], refs[-1]
    offset = offset_ref[0:1, :]
    total = part_refs[0][...].astype(F32)
    for p in part_refs[1:]:
        total = total + p[...].astype(F32)
    total = total.astype(BF16)
    low_ref[...] = total
    total = total.astype(F32)
    up_wide = spread(ks, offset, total[:RANK])
    down_wide = spread(ks, offset, total[RANK:])
    down_grad = (SCALE * dot(up_wide, x_ref[...], 1, 0)).astype(BF16)
    up_grad = (SCALE * dot(down_wide, g_ref[...], 1, 0)).astype(BF16)
    for i in range(len(ks)):
        out_refs[i][pl.ds(0, RANK), :] = down_grad[i * RANK : (i + 1) * RANK]
        out_refs[i][pl.ds(RANK, RANK), :] = up_grad[i * RANK : (i + 1) * RANK]


def collect_body(ks, me_ref, table_ref, *refs):
    in_refs, down_ref, up_ref = refs[: len(ks)], refs[-2], refs[-1]
    me = me_ref[0]
    table = table_ref[...]
    rows = SLOTS * RANK
    row = lax.broadcasted_iota(I32, (rows, RANK), 0)
    col = lax.broadcasted_iota(I32, (rows, RANK), 1)
    place = jnp.concatenate(
        [(row == (wanted(me, k, table) - 1) * RANK + col).astype(F32).astype(BF16) for k in ks], axis=1
    )
    down = jnp.concatenate([r[pl.ds(0, RANK), :] for r in in_refs], axis=0)
    up = jnp.concatenate([r[pl.ds(RANK, RANK), :] for r in in_refs], axis=0)
    down_ref[...] = dot(place, down, 1, 0)
    up_ref[...] = dot(place, up, 1, 0)


def base_body(tile, loads, adds, at_ref, *refs):
    refs = list(refs)
    if not loads:
        g = refs.pop(0)
    w_ref = refs.pop(0)
    late = refs[: loads + adds]
    out_ref, *inner, held, sems = refs[loads + adds :]
    width = out_ref.shape[1]
    first = at_ref[0] * width
    copies = [
        pltpu.make_async_copy(
            w_ref.at[pl.ds(pl.multiple_of(first + i * tile, tile), tile), :], held.at[i], sems.at[i]
        )
        for i in range(width // tile)
    ]
    others = [
        pltpu.make_async_copy(a, inner[i], sems.at[len(copies) + i]) for i, a in enumerate(late)
    ]
    if loads:
        others[0].start()
        g = inner[0]
    for c in copies:
        c.start()
    for c in others[loads:]:
        c.start()
    if loads:
        others[0].wait()
    for i, c in enumerate(copies):
        c.wait()
        columns = pl.ds(i * tile, tile)
        total = dot(g[...], held[i], 1, 1).astype(BF16)
        if i == 0:
            for o in others[loads:]:
                o.wait()
        for t in inner[loads:]:
            total = (total.astype(F32) + t[:, columns].astype(F32)).astype(BF16)
        out_ref[:, columns] = total


def base_product(gradient, weight, at, width, terms=(), loads=False, after=(), tile=512):
    tokens, depth = gradient.shape
    tiles = width // tile
    late = (gradient,) * loads + terms
    return call(
        functools.partial(base_body, tile, int(loads), len(terms)),
        sds((tokens, width), BF16),
        int(not loads),
        1,
        1 + len(late),
        scratch=[pltpu.VMEM((tokens, depth), BF16)] * len(late)
        + [pltpu.VMEM((tiles, tile, depth), BF16), pltpu.SemaphoreType.DMA((tiles + len(late),))],
        flops=2 * tokens * depth * width,
        moved=2 * depth * width,
        vmem=8,
    )(at, *((gradient,) * (not loads)), weight, *late, after=after)


def finish_body(ks, tile, at_ref, offset_ref, low_ref, *refs):
    map_refs, refs = refs[: len(ks)], refs[len(ks) :]
    g_ref, w_ref, near_ref, far_ref, out_ref, token_ref, near, far, held, sems = refs
    depth, width = held.shape[2], out_ref.shape[1]
    tiles = width // tile
    first = at_ref[0] * width
    copies = [
        pltpu.make_async_copy(
            w_ref.at[pl.ds(pl.multiple_of(first + i * tile, tile), tile), :], held.at[i], sems.at[i]
        )
        for i in range(tiles)
    ]
    terms = [
        pltpu.make_async_copy(near_ref, near, sems.at[tiles]),
        pltpu.make_async_copy(far_ref, far, sems.at[tiles + 1]),
    ]
    for c in copies + terms:
        c.start()
    down_maps = jnp.concatenate([m[pl.ds(RANK, RANK), :] for m in map_refs], axis=0)
    up_wide = spread(ks, offset_ref[0:1, :], low_ref[pl.ds(0, RANK), :].astype(F32))
    for i, c in enumerate(copies):
        c.wait()
        at = slice(i * tile, (i + 1) * tile)
        total = dot(g_ref[...], held[i], 1, 1).astype(BF16).astype(F32)
        if i == 0:
            for t in terms:
                t.wait()
        total = total + near[:, at].astype(F32) + far[:, at].astype(F32)
        lora = (SCALE * dot(up_wide, down_maps[:, at], 0, 0)).astype(BF16).astype(F32)
        out_ref[:, at] = (total + lora).astype(BF16)
    token_ref[...] = jnp.zeros_like(token_ref)


def on_device(x, g, weight, down_maps, up_maps, slot_table, group_index, group_length):
    tokens, width = x.shape
    n = lax.axis_size("adapter")
    tensor = lax.axis_size("tensor")
    groups = group_index.shape[1]
    ks = tuple(range(n - 1, n // 2 - 1, -1)) + (0,) + tuple(range(n // 2 - 1, 0, -1))
    weight, slot_table, group_index, group_length, g_hbm = (
        pltpu.with_memory_space_constraint(a, pltpu.HBM)
        for a in (weight, slot_table, group_index, group_length, g)
    )
    me = lax.axis_index("adapter").astype(I32).reshape(1)
    part = lax.axis_index("tensor").astype(I32)

    asked, offset = call(
        functools.partial(request_body, n, groups, tokens),
        (sds((n, LANES), I32), sds((SLOTS, tokens), I32)),
        0,
        4,
    )(me, slot_table, group_index, group_length)

    def product(k, *after, terms=(), loads=False):
        at = jnp.bitwise_xor(part, k).reshape(1)
        terms = tuple(pltpu.with_memory_space_constraint(t, pltpu.HBM) for t in terms)
        return base_product(g_hbm if loads else g, weight, at, width, terms, loads, after)

    wide = sds((tokens, width), BF16)
    table, tables, hop = asked, [], n // 2
    while hop:
        table = table + exchange(table, "adapter", hop)
        tables.append(table)
        hop //= 2
    far_other = product(3, asked, loads=True)
    far_got = exchange(far_other, "tensor", 1)
    near_other = product(1, far_other, loads=False)
    near_got = exchange(near_other, "tensor", 1)
    far_sum = product(2, tables[0], terms=(far_got,), loads=True)
    across = exchange(far_sum, "tensor", 2)
    sent = call(
        functools.partial(select_body, ks),
        tuple(sds((2 * RANK, width), BF16) for _ in ks),
        3,
        1,
    )(me, table, down_maps, up_maps, after=(far_sum,))
    order = [k for k in ks if k]
    sent = dict(zip(ks, sent))
    got = {k: exchange(sent[k], "adapter", k) for k in order}
    got[0] = sent[0]
    maps = [got[k] for k in ks]
    own_part = call(
        functools.partial(project_body, ks), sds((2 * RANK, tokens), BF16), 3 + n, flops=5000000000
    )(offset, x, g, *maps, after=())
    parts = [own_part] + [exchange(own_part, "tensor", k) for k in range(1, tensor)]
    out = call(
        functools.partial(gradient_body, ks, tensor),
        tuple(sds((2 * RANK, width), BF16) for _ in ks) + (sds((2 * RANK, tokens), BF16),),
        3 + tensor,
        flops=5000000000,
    )(offset, x, g, *parts, after=(across,))
    low = out[-1]
    sums = dict(zip(ks, out))
    got = {k: exchange(sums[k], "adapter", k) for k in order}
    got[0] = sums[0]
    back = [got[k] for k in ks]
    near_got, across = (pltpu.with_memory_space_constraint(a, pltpu.HBM) for a in (near_got, across))
    tile = width // 2
    input_gradient, finished = call(
        functools.partial(finish_body, ks, tile),
        (wide, sds((8, LANES), F32)),
        2 + n + 1,
        1,
        3,
        scratch=[pltpu.VMEM((tokens, width), BF16)] * 2
        + [pltpu.VMEM((2, tile, width), BF16), pltpu.SemaphoreType.DMA((4,))],
        flops=2 * tokens * width * width,
    )(part.reshape(1), offset, low, *maps, g, weight, near_got, across)
    down_grad, up_grad = call(
        functools.partial(collect_body, ks),
        (sds((SLOTS * RANK, width), F32), sds((SLOTS * RANK, width), F32)),
        1 + n,
        1,
    )(me, table, *back, after=(finished,))
    return input_gradient, down_grad, up_grad


def solution(mesh):
    in_specs = (
        P("adapter", "tensor"),
        P("adapter", "tensor"),
        P(None, "tensor"),
        P("adapter", "tensor"),
        P("adapter", "tensor"),
        P(),
        P("adapter", None),
        P("adapter", None),
    )
    out_specs = (P("adapter", "tensor"), P("adapter", "tensor"), P("adapter", "tensor"))
    return jax.shard_map(
        on_device, mesh=mesh, in_specs=in_specs, out_specs=out_specs, check_vma=False
    )
```

```python
import functools

import jax
import jax.numpy as jnp
from jax import lax
from jax.experimental import pallas as pl
from jax.experimental.pallas import tpu as pltpu
from jax.sharding import PartitionSpec as P

RANK = 16
SLOTS = 8
SCALE = 2.0
LANES = 128
VMEM = pl.BlockSpec(memory_space=pltpu.VMEM)
SMEM = pl.BlockSpec(memory_space=pltpu.SMEM)
F32 = jnp.float32
BF16 = jnp.bfloat16
I32 = jnp.int32


def dot(a, b, ca, cb):
    return lax.dot_general(a, b, (((ca,), (cb,)), ((), ())), preferred_element_type=F32)


def exchange(x, axis, k):
    return lax.ppermute(x, axis, [(i, i ^ k) for i in range(lax.axis_size(axis))])


def sds(shape, dtype):
    return jax.ShapeDtypeStruct(shape, dtype)


def call(body, outs, n_vmem, n_smem=0, n_hbm=0, scratch=(), flops=0, moved=0, vmem=16):
    def run(*operands, after=()):
        tokens = len(after)
        at = n_smem + n_vmem + n_hbm

        def wrapped(*refs):
            body(*refs[:at], *refs[at + tokens :])

        return pl.pallas_call(
            wrapped,
            name=getattr(body, "func", body).__name__,
            out_shape=outs,
            in_specs=[SMEM] * n_smem
            + [VMEM] * n_vmem
            + [pl.BlockSpec(memory_space=pltpu.HBM)] * n_hbm
            + [pl.BlockSpec(memory_space=pl.ANY)] * tokens,
            out_specs=jax.tree.map(lambda _: VMEM, outs),
            scratch_shapes=scratch,
            cost_estimate=pl.CostEstimate(flops=flops, bytes_accessed=moved, transcendentals=0),
            compiler_params=pltpu.CompilerParams(vmem_limit_bytes=vmem * 2**20),
        )(*operands, *after)

    return run


def request_body(n, groups, tokens, me_ref, slots_ref, index_ref, length_ref, asked_ref, offset_ref):
    me = me_ref[0]
    lane = lax.broadcasted_iota(I32, (n, LANES), 1)
    row = lax.broadcasted_iota(I32, (n, LANES), 0)
    token = lax.broadcasted_iota(I32, (SLOTS, tokens), 1)
    asked = jnp.zeros((n, LANES), I32)
    offset = jnp.zeros((SLOTS, tokens), I32)
    end = jnp.int32(0)
    for g in range(groups):
        slot = slots_ref[index_ref[0, g]]
        owner = lax.shift_right_logical(slot, 3)
        local = jnp.bitwise_and(slot, SLOTS - 1)
        asked = jnp.where((lane == owner) & (row == me), local + 1, asked)
        offset = jnp.where(token >= end, jnp.bitwise_xor(owner, me), offset)
        end = end + length_ref[0, g]
    asked_ref[...] = asked
    offset_ref[...] = offset


def wanted(me, k, table):
    lane = lax.broadcasted_iota(I32, table.shape, 1)
    row = lax.broadcasted_iota(I32, table.shape, 0)
    mine = jnp.where((lane == me) & (row == jnp.bitwise_xor(me, k)), table, 0)
    return jnp.sum(jnp.sum(mine, axis=1, keepdims=True), axis=0, keepdims=True)


def select_body(ks, me_ref, table_ref, down_ref, up_ref, *out_refs):
    me = me_ref[0]
    table = table_ref[...]
    rows = SLOTS * RANK
    col = lax.broadcasted_iota(I32, (RANK, rows), 1)
    row = lax.broadcasted_iota(I32, (RANK, rows), 0)
    picks = [
        (col == (wanted(me, k, table) - 1) * RANK + row).astype(F32).astype(BF16) for k in ks
    ]
    pick = jnp.concatenate(picks, axis=0)
    up = dot(pick, up_ref[...], 1, 0).astype(BF16)
    down = dot(pick, down_ref[...], 1, 0).astype(BF16)
    for i in range(len(ks)):
        out_refs[i][pl.ds(0, RANK), :] = up[i * RANK : (i + 1) * RANK]
        out_refs[i][pl.ds(RANK, RANK), :] = down[i * RANK : (i + 1) * RANK]


def project_body(ks, offset_ref, x_ref, g_ref, *refs):
    map_refs, out_ref = refs[: len(ks)], refs[len(ks)]
    offset = offset_ref[0:1, :]
    up_maps = jnp.concatenate([m[pl.ds(0, RANK), :] for m in map_refs], axis=0)
    down_maps = jnp.concatenate([m[pl.ds(RANK, RANK), :] for m in map_refs], axis=0)
    up_wide = dot(up_maps, g_ref[...], 1, 1)
    down_wide = dot(down_maps, x_ref[...], 1, 1)
    up = jnp.zeros((RANK, up_wide.shape[1]), F32)
    down = up
    for i, k in enumerate(ks):
        mask = offset == k
        up = up + jnp.where(mask, up_wide[i * RANK : (i + 1) * RANK], 0.0)
        down = down + jnp.where(mask, down_wide[i * RANK : (i + 1) * RANK], 0.0)
    out_ref[pl.ds(0, RANK), :] = up.astype(BF16)
    out_ref[pl.ds(RANK, RANK), :] = down.astype(BF16)


def spread(ks, offset, low):
    zero = jnp.zeros_like(low)
    return jnp.concatenate([jnp.where(offset == k, low, zero) for k in ks], axis=0).astype(BF16)


def gradient_body(ks, parts, offset_ref, x_ref, g_ref, *refs):
    part_refs, out_refs, low_ref = refs[:parts], refs[parts : parts + len(ks)], refs[-1]
    offset = offset_ref[0:1, :]
    total = part_refs[0][...].astype(F32)
    for p in part_refs[1:]:
        total = total + p[...].astype(F32)
    total = total.astype(BF16)
    low_ref[...] = total
    total = total.astype(F32)
    up_wide = spread(ks, offset, total[:RANK])
    down_wide = spread(ks, offset, total[RANK:])
    down_grad = (SCALE * dot(up_wide, x_ref[...], 1, 0)).astype(BF16)
    up_grad = (SCALE * dot(down_wide, g_ref[...], 1, 0)).astype(BF16)
    for i in range(len(ks)):
        out_refs[i][pl.ds(0, RANK), :] = down_grad[i * RANK : (i + 1) * RANK]
        out_refs[i][pl.ds(RANK, RANK), :] = up_grad[i * RANK : (i + 1) * RANK]


def collect_body(ks, me_ref, table_ref, *refs):
    in_refs, down_ref, up_ref = refs[: len(ks)], refs[-2], refs[-1]
    me = me_ref[0]
    table = table_ref[...]
    rows = SLOTS * RANK
    row = lax.broadcasted_iota(I32, (rows, RANK), 0)
    col = lax.broadcasted_iota(I32, (rows, RANK), 1)
    place = jnp.concatenate(
        [(row == (wanted(me, k, table) - 1) * RANK + col).astype(F32).astype(BF16) for k in ks], axis=1
    )
    down = jnp.concatenate([r[pl.ds(0, RANK), :] for r in in_refs], axis=0)
    up = jnp.concatenate([r[pl.ds(RANK, RANK), :] for r in in_refs], axis=0)
    down_ref[...] = dot(place, down, 1, 0)
    up_ref[...] = dot(place, up, 1, 0)


def base_body(tile, loads, adds, at_ref, *refs):
    refs = list(refs)
    if not loads:
        g = refs.pop(0)
    w_ref = refs.pop(0)
    late = refs[: loads + adds]
    out_ref, *inner, held, sems = refs[loads + adds :]
    width = out_ref.shape[1]
    first = at_ref[0] * width
    copies = [
        pltpu.make_async_copy(
            w_ref.at[pl.ds(pl.multiple_of(first + i * tile, tile), tile), :], held.at[i], sems.at[i]
        )
        for i in range(width // tile)
    ]
    others = [
        pltpu.make_async_copy(a, inner[i], sems.at[len(copies) + i]) for i, a in enumerate(late)
    ]
    if loads:
        others[0].start()
        g = inner[0]
    for c in copies:
        c.start()
    for c in others[loads:]:
        c.start()
    if loads:
        others[0].wait()
    for i, c in enumerate(copies):
        c.wait()
        columns = pl.ds(i * tile, tile)
        total = dot(g[...], held[i], 1, 1).astype(BF16)
        if i == 0:
            for o in others[loads:]:
                o.wait()
        for t in inner[loads:]:
            total = (total.astype(F32) + t[:, columns].astype(F32)).astype(BF16)
        out_ref[:, columns] = total


def base_product(gradient, weight, at, width, terms=(), loads=False, after=(), tile=512):
    tokens, depth = gradient.shape
    tiles = width // tile
    late = (gradient,) * loads + terms
    return call(
        functools.partial(base_body, tile, int(loads), len(terms)),
        sds((tokens, width), BF16),
        int(not loads),
        1,
        1 + len(late),
        scratch=[pltpu.VMEM((tokens, depth), BF16)] * len(late)
        + [pltpu.VMEM((tiles, tile, depth), BF16), pltpu.SemaphoreType.DMA((tiles + len(late),))],
        flops=2 * tokens * depth * width,
        moved=2 * depth * width,
        vmem=8,
    )(at, *((gradient,) * (not loads)), weight, *late, after=after)


def finish_body(ks, tile, at_ref, offset_ref, low_ref, *refs):
    map_refs, refs = refs[: len(ks)], refs[len(ks) :]
    g_ref, w_ref, near_ref, far_ref, out_ref, token_ref, near, far, held, sems = refs
    depth, width = held.shape[2], out_ref.shape[1]
    tiles = width // tile
    first = at_ref[0] * width
    copies = [
        pltpu.make_async_copy(
            w_ref.at[pl.ds(pl.multiple_of(first + i * tile, tile), tile), :], held.at[i], sems.at[i]
        )
        for i in range(tiles)
    ]
    terms = [
        pltpu.make_async_copy(near_ref, near, sems.at[tiles]),
        pltpu.make_async_copy(far_ref, far, sems.at[tiles + 1]),
    ]
    for c in copies + terms:
        c.start()
    down_maps = jnp.concatenate([m[pl.ds(RANK, RANK), :] for m in map_refs], axis=0)
    up_wide = spread(ks, offset_ref[0:1, :], low_ref[pl.ds(0, RANK), :].astype(F32))
    for i, c in enumerate(copies):
        c.wait()
        at = slice(i * tile, (i + 1) * tile)
        total = dot(g_ref[...], held[i], 1, 1).astype(BF16).astype(F32)
        if i == 0:
            for t in terms:
                t.wait()
        total = total + near[:, at].astype(F32) + far[:, at].astype(F32)
        lora = (SCALE * dot(up_wide, down_maps[:, at], 0, 0)).astype(BF16).astype(F32)
        out_ref[:, at] = (total + lora).astype(BF16)
    token_ref[...] = jnp.zeros_like(token_ref)


def on_device(x, g, weight, down_maps, up_maps, slot_table, group_index, group_length):
    tokens, width = x.shape
    n = lax.axis_size("adapter")
    tensor = lax.axis_size("tensor")
    groups = group_index.shape[1]
    ks = tuple(range(n - 1, n // 2 - 1, -1)) + (0,) + tuple(range(n // 2 - 1, 0, -1))
    weight, slot_table, group_index, group_length, g_hbm = (
        pltpu.with_memory_space_constraint(a, pltpu.HBM)
        for a in (weight, slot_table, group_index, group_length, g)
    )
    me = lax.axis_index("adapter").astype(I32).reshape(1)
    part = lax.axis_index("tensor").astype(I32)

    asked, offset = call(
        functools.partial(request_body, n, groups, tokens),
        (sds((n, LANES), I32), sds((SLOTS, tokens), I32)),
        0,
        4,
    )(me, slot_table, group_index, group_length)

    def product(k, *after, terms=(), loads=False):
        at = jnp.bitwise_xor(part, k).reshape(1)
        terms = tuple(pltpu.with_memory_space_constraint(t, pltpu.HBM) for t in terms)
        return base_product(g_hbm if loads else g, weight, at, width, terms, loads, after)

    wide = sds((tokens, width), BF16)
    table, tables, hop = asked, [], n // 2
    while hop > 2:
        table = table + exchange(table, "adapter", hop)
        tables.append(table)
        hop //= 2
    table = table + sum(exchange(table, "adapter", k) for k in (2, 3, 1))
    far_other = product(3, asked, loads=True)
    far_got = exchange(far_other, "tensor", 1)
    near_other = product(1, far_other, loads=False)
    near_got = exchange(near_other, "tensor", 1)
    far_sum = product(2, tables[0], terms=(far_got,), loads=True)
    across = exchange(far_sum, "tensor", 2)
    sent = call(
        functools.partial(select_body, ks),
        tuple(sds((2 * RANK, width), BF16) for _ in ks),
        3,
        1,
    )(me, table, down_maps, up_maps, after=(far_sum,))
    order = [k for k in ks if k]
    sent = dict(zip(ks, sent))
    got = {k: exchange(sent[k], "adapter", k) for k in order}
    got[0] = sent[0]
    maps = [got[k] for k in ks]
    own_part = call(
        functools.partial(project_body, ks), sds((2 * RANK, tokens), BF16), 3 + n, flops=5000000000
    )(offset, x, g, *maps, after=())
    parts = [own_part] + [exchange(own_part, "tensor", k) for k in range(1, tensor)]
    out = call(
        functools.partial(gradient_body, ks, tensor),
        tuple(sds((2 * RANK, width), BF16) for _ in ks) + (sds((2 * RANK, tokens), BF16),),
        3 + tensor,
        flops=5000000000,
    )(offset, x, g, *parts, after=(across,))
    low = out[-1]
    sums = dict(zip(ks, out))
    got = {k: exchange(sums[k], "adapter", k) for k in order}
    got[0] = sums[0]
    back = [got[k] for k in ks]
    near_got, across = (pltpu.with_memory_space_constraint(a, pltpu.HBM) for a in (near_got, across))
    tile = width // 2
    input_gradient, finished = call(
        functools.partial(finish_body, ks, tile),
        (wide, sds((8, LANES), F32)),
        2 + n + 1,
        1,
        3,
        scratch=[pltpu.VMEM((tokens, width), BF16)] * 2
        + [pltpu.VMEM((2, tile, width), BF16), pltpu.SemaphoreType.DMA((4,))],
        flops=2 * tokens * width * width,
    )(part.reshape(1), offset, low, *maps, g, weight, near_got, across)
    down_grad, up_grad = call(
        functools.partial(collect_body, ks),
        (sds((SLOTS * RANK, width), F32), sds((SLOTS * RANK, width), F32)),
        1 + n,
        1,
    )(me, table, *back, after=(finished,))
    return input_gradient, down_grad, up_grad


def solution(mesh):
    in_specs = (
        P("adapter", "tensor"),
        P("adapter", "tensor"),
        P(None, "tensor"),
        P("adapter", "tensor"),
        P("adapter", "tensor"),
        P(),
        P("adapter", None),
        P("adapter", None),
    )
    out_specs = (P("adapter", "tensor"), P("adapter", "tensor"), P("adapter", "tensor"))
    return jax.shard_map(
        on_device, mesh=mesh, in_specs=in_specs, out_specs=out_specs, check_vma=False
    )
```

```python
import functools

import jax
import jax.numpy as jnp
from jax import lax
from jax.experimental import pallas as pl
from jax.experimental.pallas import tpu as pltpu
from jax.sharding import PartitionSpec as P

RANK = 16
SLOTS = 8
SCALE = 2.0
LANES = 128
VMEM = pl.BlockSpec(memory_space=pltpu.VMEM)
SMEM = pl.BlockSpec(memory_space=pltpu.SMEM)
F32 = jnp.float32
BF16 = jnp.bfloat16
I32 = jnp.int32


def dot(a, b, ca, cb):
    return lax.dot_general(a, b, (((ca,), (cb,)), ((), ())), preferred_element_type=F32)


def exchange(x, axis, k):
    return lax.ppermute(x, axis, [(i, i ^ k) for i in range(lax.axis_size(axis))])


def sds(shape, dtype):
    return jax.ShapeDtypeStruct(shape, dtype)


def call(body, outs, n_vmem, n_smem=0, n_hbm=0, scratch=(), flops=0, moved=0, vmem=16, space=VMEM):
    def run(*operands, after=()):
        tokens = len(after)
        at = n_smem + n_vmem + n_hbm

        def wrapped(*refs):
            body(*refs[:at], *refs[at + tokens :])

        return pl.pallas_call(
            wrapped,
            name=getattr(body, "func", body).__name__,
            out_shape=outs,
            in_specs=[SMEM] * n_smem
            + [VMEM] * n_vmem
            + [pl.BlockSpec(memory_space=pltpu.HBM)] * n_hbm
            + [pl.BlockSpec(memory_space=pl.ANY)] * tokens,
            out_specs=jax.tree.map(lambda _: space, outs),
            scratch_shapes=scratch,
            cost_estimate=pl.CostEstimate(flops=flops, bytes_accessed=moved, transcendentals=0),
            compiler_params=pltpu.CompilerParams(vmem_limit_bytes=vmem * 2**20),
        )(*operands, *after)

    return run


def request_body(n, groups, tokens, me_ref, slots_ref, index_ref, length_ref, asked_ref, offset_ref):
    me = me_ref[0]
    lane = lax.broadcasted_iota(I32, (n, LANES), 1)
    row = lax.broadcasted_iota(I32, (n, LANES), 0)
    token = lax.broadcasted_iota(I32, (SLOTS, tokens), 1)
    asked = jnp.zeros((n, LANES), I32)
    offset = jnp.zeros((SLOTS, tokens), I32)
    end = jnp.int32(0)
    for g in range(groups):
        slot = slots_ref[index_ref[0, g]]
        owner = lax.shift_right_logical(slot, 3)
        local = jnp.bitwise_and(slot, SLOTS - 1)
        asked = jnp.where((lane == owner) & (row == me), local + 1, asked)
        offset = jnp.where(token >= end, jnp.bitwise_xor(owner, me), offset)
        end = end + length_ref[0, g]
    asked_ref[...] = asked
    offset_ref[...] = offset


def wanted(me, k, table):
    lane = lax.broadcasted_iota(I32, table.shape, 1)
    row = lax.broadcasted_iota(I32, table.shape, 0)
    mine = jnp.where((lane == me) & (row == jnp.bitwise_xor(me, k)), table, 0)
    return jnp.sum(jnp.sum(mine, axis=1, keepdims=True), axis=0, keepdims=True)


def select_body(ks, me_ref, table_ref, down_ref, up_ref, *out_refs):
    me = me_ref[0]
    table = table_ref[...]
    rows = SLOTS * RANK
    col = lax.broadcasted_iota(I32, (RANK, rows), 1)
    row = lax.broadcasted_iota(I32, (RANK, rows), 0)
    picks = [
        (col == (wanted(me, k, table) - 1) * RANK + row).astype(F32).astype(BF16) for k in ks
    ]
    pick = jnp.concatenate(picks, axis=0)
    up = dot(pick, up_ref[...], 1, 0).astype(BF16)
    down = dot(pick, down_ref[...], 1, 0).astype(BF16)
    for i in range(len(ks)):
        out_refs[i][pl.ds(0, RANK), :] = up[i * RANK : (i + 1) * RANK]
        out_refs[i][pl.ds(RANK, RANK), :] = down[i * RANK : (i + 1) * RANK]


def project_body(ks, offset_ref, x_ref, g_ref, *refs):
    map_refs, out_ref = refs[: len(ks)], refs[len(ks)]
    offset = offset_ref[0:1, :]
    up_maps = jnp.concatenate([m[pl.ds(0, RANK), :] for m in map_refs], axis=0)
    down_maps = jnp.concatenate([m[pl.ds(RANK, RANK), :] for m in map_refs], axis=0)
    up_wide = dot(up_maps, g_ref[...], 1, 1)
    down_wide = dot(down_maps, x_ref[...], 1, 1)
    up = jnp.zeros((RANK, up_wide.shape[1]), F32)
    down = up
    for i, k in enumerate(ks):
        mask = offset == k
        up = up + jnp.where(mask, up_wide[i * RANK : (i + 1) * RANK], 0.0)
        down = down + jnp.where(mask, down_wide[i * RANK : (i + 1) * RANK], 0.0)
    out_ref[pl.ds(0, RANK), :] = up.astype(BF16)
    out_ref[pl.ds(RANK, RANK), :] = down.astype(BF16)


def spread(ks, offset, low):
    zero = jnp.zeros_like(low)
    return jnp.concatenate([jnp.where(offset == k, low, zero) for k in ks], axis=0).astype(BF16)


def gradient_body(ks, parts, offset_ref, x_ref, g_ref, *refs):
    part_refs, out_refs, low_ref = refs[:parts], refs[parts : parts + len(ks)], refs[-1]
    offset = offset_ref[0:1, :]
    total = part_refs[0][...].astype(F32)
    for p in part_refs[1:]:
        total = total + p[...].astype(F32)
    total = total.astype(BF16)
    low_ref[...] = total
    total = total.astype(F32)
    up_wide = spread(ks, offset, total[:RANK])
    down_wide = spread(ks, offset, total[RANK:])
    down_grad = (SCALE * dot(up_wide, x_ref[...], 1, 0)).astype(BF16)
    up_grad = (SCALE * dot(down_wide, g_ref[...], 1, 0)).astype(BF16)
    for i in range(len(ks)):
        out_refs[i][pl.ds(0, RANK), :] = down_grad[i * RANK : (i + 1) * RANK]
        out_refs[i][pl.ds(RANK, RANK), :] = up_grad[i * RANK : (i + 1) * RANK]


def collect_body(ks, me_ref, table_ref, *refs):
    in_refs, (down_ref, up_ref, down_sum, up_sum, sems) = refs[: len(ks)], refs[len(ks) :]
    me = me_ref[0]
    table = table_ref[...]
    rows = SLOTS * RANK
    row = lax.broadcasted_iota(I32, (rows, RANK), 0)
    col = lax.broadcasted_iota(I32, (rows, RANK), 1)
    place = jnp.concatenate(
        [(row == (wanted(me, k, table) - 1) * RANK + col).astype(F32).astype(BF16) for k in ks], axis=1
    )
    copies = []
    for i, (held, out) in enumerate(((down_sum, down_ref), (up_sum, up_ref))):
        terms = jnp.concatenate([r[pl.ds(i * RANK, RANK), :] for r in in_refs], axis=0)
        held[...] = dot(place, terms, 1, 0)
        copies.append(pltpu.make_async_copy(held, out, sems.at[i]))
        copies[-1].start()
    for c in copies:
        c.wait()


def base_body(tile, loads, adds, at_ref, *refs):
    refs = list(refs)
    if not loads:
        g = refs.pop(0)
    w_ref = refs.pop(0)
    late = refs[: loads + adds]
    out_ref, *inner, held, sems = refs[loads + adds :]
    width = out_ref.shape[1]
    first = at_ref[0] * width
    copies = [
        pltpu.make_async_copy(
            w_ref.at[pl.ds(pl.multiple_of(first + i * tile, tile), tile), :], held.at[i], sems.at[i]
        )
        for i in range(width // tile)
    ]
    others = [
        pltpu.make_async_copy(a, inner[i], sems.at[len(copies) + i]) for i, a in enumerate(late)
    ]
    if loads:
        others[0].start()
        g = inner[0]
    for c in copies:
        c.start()
    for c in others[loads:]:
        c.start()
    if loads:
        others[0].wait()
    for i, c in enumerate(copies):
        c.wait()
        columns = pl.ds(i * tile, tile)
        total = dot(g[...], held[i], 1, 1).astype(BF16)
        if i == 0:
            for o in others[loads:]:
                o.wait()
        for t in inner[loads:]:
            total = (total.astype(F32) + t[:, columns].astype(F32)).astype(BF16)
        out_ref[:, columns] = total


def base_product(gradient, weight, at, width, terms=(), loads=False, after=(), tile=512):
    tokens, depth = gradient.shape
    tiles = width // tile
    late = (gradient,) * loads + terms
    return call(
        functools.partial(base_body, tile, int(loads), len(terms)),
        sds((tokens, width), BF16),
        int(not loads),
        1,
        1 + len(late),
        scratch=[pltpu.VMEM((tokens, depth), BF16)] * len(late)
        + [pltpu.VMEM((tiles, tile, depth), BF16), pltpu.SemaphoreType.DMA((tiles + len(late),))],
        flops=2 * tokens * depth * width,
        moved=2 * depth * width,
        vmem=8,
    )(at, *((gradient,) * (not loads)), weight, *late, after=after)


def finish_body(ks, tile, at_ref, offset_ref, low_ref, *refs):
    map_refs, refs = refs[: len(ks)], refs[len(ks) :]
    g_ref, w_ref, near_ref, far_ref, out_ref, token_ref, near, far, held, sems = refs
    depth, width = held.shape[2], out_ref.shape[1]
    tiles = width // tile
    first = at_ref[0] * width
    copies = [
        pltpu.make_async_copy(
            w_ref.at[pl.ds(pl.multiple_of(first + i * tile, tile), tile), :], held.at[i], sems.at[i]
        )
        for i in range(tiles)
    ]
    terms = [
        pltpu.make_async_copy(near_ref, near, sems.at[tiles]),
        pltpu.make_async_copy(far_ref, far, sems.at[tiles + 1]),
    ]
    for c in copies + terms:
        c.start()
    down_maps = jnp.concatenate([m[pl.ds(RANK, RANK), :] for m in map_refs], axis=0)
    up_wide = spread(ks, offset_ref[0:1, :], low_ref[pl.ds(0, RANK), :].astype(F32))
    for i, c in enumerate(copies):
        c.wait()
        at = slice(i * tile, (i + 1) * tile)
        total = dot(g_ref[...], held[i], 1, 1).astype(BF16).astype(F32)
        if i == 0:
            for t in terms:
                t.wait()
        total = total + near[:, at].astype(F32) + far[:, at].astype(F32)
        lora = (SCALE * dot(up_wide, down_maps[:, at], 0, 0)).astype(BF16).astype(F32)
        out_ref[:, at] = (total + lora).astype(BF16)
    token_ref[...] = jnp.zeros_like(token_ref)


def on_device(x, g, weight, down_maps, up_maps, slot_table, group_index, group_length):
    tokens, width = x.shape
    n = lax.axis_size("adapter")
    tensor = lax.axis_size("tensor")
    groups = group_index.shape[1]
    ks = tuple(range(n - 1, n // 2 - 1, -1)) + (0,) + tuple(range(n // 2 - 1, 0, -1))
    weight, slot_table, group_index, group_length, g_hbm = (
        pltpu.with_memory_space_constraint(a, pltpu.HBM)
        for a in (weight, slot_table, group_index, group_length, g)
    )
    me = lax.axis_index("adapter").astype(I32).reshape(1)
    part = lax.axis_index("tensor").astype(I32)

    asked, offset = call(
        functools.partial(request_body, n, groups, tokens),
        (sds((n, LANES), I32), sds((SLOTS, tokens), I32)),
        0,
        4,
    )(me, slot_table, group_index, group_length)

    def product(k, *after, terms=(), loads=False):
        at = jnp.bitwise_xor(part, k).reshape(1)
        terms = tuple(pltpu.with_memory_space_constraint(t, pltpu.HBM) for t in terms)
        return base_product(g_hbm if loads else g, weight, at, width, terms, loads, after)

    wide = sds((tokens, width), BF16)
    table, tables, hop = asked, [], n // 2
    while hop > 2:
        table = table + exchange(table, "adapter", hop)
        tables.append(table)
        hop //= 2
    table = table + sum(exchange(table, "adapter", k) for k in (2, 3, 1))
    far_other = product(3, asked, loads=True)
    far_got = exchange(far_other, "tensor", 1)
    near_other = product(1, far_other, loads=False)
    near_got = exchange(near_other, "tensor", 1)
    far_sum = product(2, tables[0], terms=(far_got,), loads=True)
    across = exchange(far_sum, "tensor", 2)
    sent = call(
        functools.partial(select_body, ks),
        tuple(sds((2 * RANK, width), BF16) for _ in ks),
        3,
        1,
    )(me, table, down_maps, up_maps, after=(far_sum,))
    order = [k for k in ks if k]
    sent = dict(zip(ks, sent))
    got = {k: exchange(sent[k], "adapter", k) for k in order}
    got[0] = sent[0]
    maps = [got[k] for k in ks]
    own_part = call(
        functools.partial(project_body, ks), sds((2 * RANK, tokens), BF16), 3 + n, flops=5000000000
    )(offset, x, g, *maps, after=())
    parts = [own_part] + [exchange(own_part, "tensor", k) for k in range(1, tensor)]
    out = call(
        functools.partial(gradient_body, ks, tensor),
        tuple(sds((2 * RANK, width), BF16) for _ in ks) + (sds((2 * RANK, tokens), BF16),),
        3 + tensor,
        flops=5000000000,
    )(offset, x, g, *parts, after=(across,))
    low = out[-1]
    sums = dict(zip(ks, out))
    got = {k: exchange(sums[k], "adapter", k) for k in order}
    got[0] = sums[0]
    back = [got[k] for k in ks]
    near_got, across = (pltpu.with_memory_space_constraint(a, pltpu.HBM) for a in (near_got, across))
    tile = width // 2
    input_gradient, finished = call(
        functools.partial(finish_body, ks, tile),
        (wide, sds((8, LANES), F32)),
        2 + n + 1,
        1,
        3,
        scratch=[pltpu.VMEM((tokens, width), BF16)] * 2
        + [pltpu.VMEM((2, tile, width), BF16), pltpu.SemaphoreType.DMA((4,))],
        flops=2 * tokens * width * width,
    )(part.reshape(1), offset, low, *maps, g, weight, near_got, across)
    down_grad, up_grad = call(
        functools.partial(collect_body, ks),
        (sds((SLOTS * RANK, width), F32), sds((SLOTS * RANK, width), F32)),
        1 + n,
        1,
        scratch=[pltpu.VMEM((SLOTS * RANK, width), F32)] * 2 + [pltpu.SemaphoreType.DMA((2,))],
        space=pl.BlockSpec(memory_space=pltpu.HBM),
    )(me, table, *back, after=(finished,))
    return input_gradient, down_grad, up_grad


def solution(mesh):
    in_specs = (
        P("adapter", "tensor"),
        P("adapter", "tensor"),
        P(None, "tensor"),
        P("adapter", "tensor"),
        P("adapter", "tensor"),
        P(),
        P("adapter", None),
        P("adapter", None),
    )
    out_specs = (P("adapter", "tensor"), P("adapter", "tensor"), P("adapter", "tensor"))
    return jax.shard_map(
        on_device, mesh=mesh, in_specs=in_specs, out_specs=out_specs, check_vma=False
    )
```
